32 devices in a mesh: tok: 8 (over z, x), head: 4 (over y, core).
Axes of the slice: x: 2, y: 2, z: 4, core: 2. Of those that a mesh axis runs over, the one named last changes fastest.
Arguments:
- embeddings: bfloat16 [1024, 4096], P('tok'), may hold values from -6 to 6
- norm_gain: bfloat16 [4096], replicated, may hold values from 0.099609375 to 1.8984375
- query_key_value_weight: bfloat16 [4096, 6144], P(None, 'head'), may hold values from -0.09375 to 0.09375
- embed_table: bfloat16 [65536, 4096], P('tok', 'head'), may hold values from -6 to 6
- rotated_cache_pages: bfloat16 [8, 8, 256, 2048], P('tok', None, None, 'head'), may hold values from -300 to 300
- page_owner_device: int32 [8, 8], P('tok'), may hold values from 0 to 7, each once within a row
- cached_length: int32 [8], P('tok'), may hold values from 2 to 2048, as said below
- vocab_shard: int32 [1024, 1], P('tok'), may hold values from 0 to 7; in each aligned block of 128 rows (0 to 127, 128 to 255, ...) at most 32 rows name the same one
- shard_row: int32 [1024], P('tok'), may hold values from 0 to 8191
- accept: int32 [1024], P('tok'), may hold values from 0 to 1, as said below
Outputs:
- out_first: bfloat16 [1024, 4096], P('tok', 'head')
- out_second: bfloat16 [1024, 4096], P('tok', 'head')
The draws below stay inside these ranges and needn't reach their ends.
Inputs may be any that keep to these rules, and one draw needn't show every extreme that they name: `page_owner_device`: each row names every device of the tok axis once. `cached_length`: some request has exactly 2048 cached positions. `vocab_shard`: at most 32 of the 128 tokens of one request name the same shard, and some shard is named that often. `accept`: at most 32 accepted tokens in one request's block; some block has exactly 32.
All inputs are finite; a program needn't handle non-finite values.
Results may differ from the reference program's by a relative error of at most 0.017.
The reference program's roundings to bfloat16 on the way count: a program that leaves them out, or rounds other values in their place, can miss the bound.
Values may be sent and summed in bfloat16 or wider, within the bound.
A program may use at most 128 MiB of HBM per device.

```python
import math
import jax
import jax.numpy as jnp
import numpy as np
from jax import lax

MODEL_WIDTH = 4096
QUERY_HEADS = 32
KEY_VALUE_HEADS = 8
HEAD_SIZE = 128
VOCAB = 65536
BLOCK_TOKENS = 128
PAGE_POSITIONS = 256
REQUEST_COUNT = 8
TOKENS = 1024
CAP = 32
ACC = 32
SHARD_ROWS = 8192


def draw_rotated_cache_pages(key, part):
    key_first = jax.random.fold_in(key, 0)
    complete_shape = (REQUEST_COUNT, REQUEST_COUNT, PAGE_POSITIONS, KEY_VALUE_HEADS, 2, HEAD_SIZE)
    gaussian_draw = jnp.clip(jax.random.normal(key_first, complete_shape, jnp.float32), -6.0, 6.0)
    return gaussian_draw.reshape(REQUEST_COUNT, REQUEST_COUNT, PAGE_POSITIONS, KEY_VALUE_HEADS * 2 * HEAD_SIZE).astype(jnp.bfloat16)


def draw_cached_length(key, part):
    key_first, key_second = jax.random.split(key)
    longest = PAGE_POSITIONS * REQUEST_COUNT
    lengths = jax.random.randint(key_first, (REQUEST_COUNT,), 2, longest + 1)
    chosen = jax.random.randint(key_second, (), 0, REQUEST_COUNT)
    return jnp.where(jnp.arange(REQUEST_COUNT) == chosen, longest, lengths).astype(jnp.int32)


def draw_accept(key, part):
    key_first, key_second, key_slice_three = jax.random.split(key, 3)
    counts = jax.random.randint(key_first, (REQUEST_COUNT,), max(ACC // 2, 1), ACC + 1)
    chosen = jax.random.randint(key_second, (), 0, REQUEST_COUNT)
    counts = jnp.where(jnp.arange(REQUEST_COUNT) == chosen, ACC, counts)
    scores = jax.random.randint(key_slice_three, (REQUEST_COUNT, BLOCK_TOKENS), 0, 1048576) * BLOCK_TOKENS + jnp.arange(BLOCK_TOKENS)[None, :]
    ranking = jnp.argsort(jnp.argsort(scores, axis=1), axis=1)
    return (ranking < counts[:, None]).astype(jnp.int32).reshape(TOKENS)


def with_ends(values, rng, smallest, top_value):
    longest = values.shape.index(max(values.shape))
    spots = []
    for shift in (0, 1):
        where = [jax.random.randint(jax.random.fold_in(rng, axis), (), 0, length) for axis, length in enumerate(values.shape)]
        where[longest] = (where[longest] + shift) % values.shape[longest]
        spots.append(tuple(where))
    return values.at[spots[0]].set(smallest).at[spots[1]].set(top_value)


def steps_of(rng, shape, pieces, least, top_value):
    factor_of = 1.0
    for axis_at, blocks in pieces:
        steps = jax.random.uniform(jax.random.fold_in(jax.random.fold_in(rng, 6), axis_at), (blocks,), jnp.float32, least / len(pieces), top_value / len(pieces))
        factor_of = factor_of * jnp.repeat(jnp.exp(steps), shape[axis_at] // blocks).reshape((-1,) + (1,) * (len(shape) - 1 - axis_at))
    return factor_of


def deal_out(own_key, own, number, rows, count, top, most, slope):
    order = jax.random.permutation(own_key, count)
    packed, ordinary = portions_of(count, rows * top, most, slope, True), portions_of(count, rows * top, most, slope, False)
    places = jnp.arange(count)

    def named(tallies, turn):
        used = int((tallies > 0).sum())
        fixed = max(1, used // 4)
        shifted = fixed + (places - fixed + turn * (used - fixed)) % max(1, count - fixed)
        return jnp.zeros((count,), jnp.int32).at[order[jnp.where(places < fixed, places, shifted)]].set(jnp.asarray(tallies, jnp.int32))

    tallies = jnp.where(number % 4 == 0, named(packed, number // 4), named(ordinary, number - number // 4 - 1))
    mixed = jax.random.permutation(jax.random.fold_in(own, 3), count)
    giver, receiver = mixed[0:count // 2 * 2:2], mixed[1:count // 2 * 2:2]
    slack = jnp.minimum(tallies[giver] - 1, most - tallies[receiver]) // 2
    slack = jnp.where((giver == order[0]) | (receiver == order[0]) | (tallies[receiver] == 0), 0, jnp.maximum(slack, 0))
    shifted = jax.random.randint(jax.random.fold_in(own, 4), (count // 2,), 0, 1 << 20) % (slack + 1)
    tallies = tallies.at[giver].add(-shifted).at[receiver].add(shifted)
    items = jnp.searchsorted(jnp.cumsum(tallies), jnp.arange(rows * top), side="right").astype(jnp.int32)
    table = items.reshape(top, rows).T
    table = table[jax.random.permutation(jax.random.fold_in(own, 1), rows)]
    turn = jax.random.randint(jax.random.fold_in(own, 2), (rows, 1), 0, top)
    return jnp.take_along_axis(table, (jnp.arange(top)[None, :] + turn) % top, axis=1)


def portions_of(count, total, limit, lean, full):
    loads = [(1 << 20) // math.isqrt(rank ** lean) + 1 for rank in range(1, count + 1)]
    largest = limit if full else min(limit, max(-(-total // count), total * loads[0] // sum(loads)))
    least = 1 if total - largest >= count - 1 else 0
    given, spare = [largest] + [least] * (count - 1), total - largest - least * (count - 1)
    while spare > 0:
        free = [i for i in range(1, count) if given[i] < largest] or [i for i in range(1, count) if given[i] < limit]
        whole, budget = sum([loads[i] for i in free]), spare
        for i in free:
            extra = min(limit - given[i], max(1, budget * loads[i] // whole), spare)
            given[i] = given[i] + extra
            spare = spare - extra
    return np.array(given)


def bell_draw(own_key, extent, deviation, reach, cuts=(), held_as=jnp.bfloat16):
    drawn = jax.random.normal(own_key, extent, jnp.float32) * deviation
    if len(cuts) > 0:
        drawn = steps_of(own_key, extent, cuts, -0.22, 0.18) * drawn
    return jnp.clip(drawn, min=-reach, max=reach).astype(held_as)


def setup_inputs(seed: int = 0) -> dict:
    keys = jax.random.split(jax.random.key(seed), 11)
    embeddings = bell_draw(keys[0], (TOKENS, MODEL_WIDTH), 1.0, 6.0, ((0, 8),))
    norm_gain = jnp.clip(1.0 + 0.18 * jax.random.normal(keys[1], (MODEL_WIDTH,), jnp.float32), 0.099609375, 1.8984375).astype(jnp.bfloat16)
    query_key_value_weight = bell_draw(keys[2], (MODEL_WIDTH, KEY_VALUE_HEADS * (QUERY_HEADS // KEY_VALUE_HEADS + 2) * HEAD_SIZE), MODEL_WIDTH ** -0.5, 0.09375, ((1, 4),))
    embed_table = bell_draw(keys[3], (VOCAB, MODEL_WIDTH), 1.0, 6.0, ((0, 8), (1, 4)))
    rotated_cache_pages = draw_rotated_cache_pages(jax.random.fold_in(keys[10], 71), 0)
    page_owner_device = jax.vmap(lambda own: jax.random.permutation(own, REQUEST_COUNT))(jax.random.split(keys[5], REQUEST_COUNT)).reshape((REQUEST_COUNT, REQUEST_COUNT)).astype(jnp.int32)
    cached_length = draw_cached_length(jax.random.fold_in(keys[10], 71), 0)
    vocab_shard_keys = jax.random.split(jax.random.fold_in(keys[7], 1), TOKENS // BLOCK_TOKENS)
    vocab_shard_turns = jax.random.permutation(jax.random.fold_in(keys[7], 3), TOKENS // BLOCK_TOKENS)
    vocab_shard = jax.vmap(lambda own, number: deal_out(jax.random.fold_in(keys[7], 2), own, number, BLOCK_TOKENS, REQUEST_COUNT, 1, CAP, 1))(vocab_shard_keys, vocab_shard_turns).reshape((TOKENS, 1))
    shard_row = with_ends(jax.random.randint(keys[8], (TOKENS,), 0, SHARD_ROWS), jax.random.fold_in(keys[8], 1), 0, SHARD_ROWS - 1).astype(jnp.int32)
    accept = draw_accept(jax.random.fold_in(keys[10], 71), 0)
    return dict(embeddings=embeddings, norm_gain=norm_gain, query_key_value_weight=query_key_value_weight, embed_table=embed_table, rotated_cache_pages=rotated_cache_pages, page_owner_device=page_owner_device, cached_length=cached_length, vocab_shard=vocab_shard, shard_row=shard_row, accept=accept)


THETA = 500000.0

def angles(positions):
    steps_half = jnp.arange(HEAD_SIZE // 2, dtype=jnp.float32)
    frequency = THETA ** (-(steps_half * 2.0) / HEAD_SIZE)
    return positions.astype(jnp.float32)[:, None] * frequency[None, :]

def rotate(vectors, turning):
    half_width = vectors.shape[-1] // 2
    former = vectors[..., :half_width]
    latter = vectors[..., half_width:]
    cosine = jnp.cos(turning)
    sine_of = jnp.sin(turning)
    return jnp.concatenate([former * cosine - latter * sine_of, latter * cosine + former * sine_of], axis=-1)

def project(inputs, norm_gain, query_key_value_weight, positions):
    widened = inputs.astype(jnp.float32)
    inverse = lax.rsqrt(lax.optimization_barrier(jnp.mean(widened * widened, axis=-1, keepdims=True)) + 1e-05)
    normed = (widened * inverse * norm_gain.astype(jnp.float32)).astype(jnp.bfloat16)
    combined = jnp.dot(normed, query_key_value_weight, preferred_element_type=jnp.float32)
    heads_per_group = QUERY_HEADS // KEY_VALUE_HEADS
    combined = combined.reshape(inputs.shape[0], -1, heads_per_group + 2, HEAD_SIZE)
    turning = angles(positions)[:, None, None, :]
    query_vectors = rotate(combined[:, :, :heads_per_group], turning).astype(jnp.bfloat16)
    block_keys = rotate(combined[:, :, heads_per_group:heads_per_group + 1], turning)[:, :, 0].astype(jnp.bfloat16)
    block_values = combined[:, :, heads_per_group + 1].astype(jnp.bfloat16)
    return (query_vectors, block_keys, block_values)

def attend(query_vectors, block_keys, block_values, page_keys, page_values, usable):
    factor = 1.0 / math.sqrt(HEAD_SIZE)
    query_wide = query_vectors.astype(jnp.float32)
    scores_cache = jnp.einsum('bgqd,kgd->gqbk', query_wide, page_keys.astype(jnp.float32)) * factor
    scores_cache = jnp.where(usable[None, None, None, :], scores_cache, -1e+30)
    scores_block = jnp.einsum('bgqd,cgd->gqbc', query_wide, block_keys.astype(jnp.float32)) * factor
    highest = jnp.maximum(lax.optimization_barrier(jnp.max(scores_cache, axis=-1)), lax.optimization_barrier(jnp.max(scores_block, axis=-1)))[..., None]
    exp_cache = jnp.exp(scores_cache - highest)
    exp_block = jnp.exp(scores_block - highest)
    totals = lax.optimization_barrier(jnp.sum(exp_cache, axis=-1)) + lax.optimization_barrier(jnp.sum(exp_block, axis=-1))
    weights_cache = lax.optimization_barrier(exp_cache.astype(jnp.bfloat16)).astype(jnp.float32)
    weights_block = lax.optimization_barrier(exp_block.astype(jnp.bfloat16)).astype(jnp.float32)
    combined = jnp.einsum('gqbk,kgd->bgqd', weights_cache, page_values.astype(jnp.float32))
    combined = combined + jnp.einsum('gqbc,cgd->bgqd', weights_block, block_values.astype(jnp.float32))
    result = combined / jnp.transpose(totals, (2, 0, 1))[..., None]
    return result.astype(jnp.bfloat16).reshape(query_vectors.shape[0], -1)

def reference(embeddings, norm_gain, query_key_value_weight, embed_table, rotated_cache_pages, page_owner_device, cached_length, vocab_shard, shard_row, accept):
    offsets = jnp.arange(BLOCK_TOKENS, dtype=jnp.int32)
    positions = (cached_length[:, None] + offsets[None, :]).reshape(-1)
    chosen_ids = (vocab_shard[:, 0] * SHARD_ROWS + shard_row).astype(jnp.int32)
    replaced = jnp.where(accept[:, None] == 1, jnp.take(embed_table, chosen_ids, axis=0), embeddings)
    page_spots = jnp.arange(PAGE_POSITIONS, dtype=jnp.int32)
    key_spots = (jnp.arange(REQUEST_COUNT, dtype=jnp.int32)[:, None] * PAGE_POSITIONS + page_spots[None, :]).reshape(-1)
    heads_per_group = QUERY_HEADS // KEY_VALUE_HEADS
    results = []
    for inputs in (embeddings, replaced):
        query_vectors, block_keys, block_values = project(inputs, norm_gain, query_key_value_weight, positions)

        def request(packed_pages):
            query_rows, key_rows, value_rows, holder_devices, length, request_number = packed_pages
            page_row_entries = rotated_cache_pages[holder_devices, request_number].reshape(REQUEST_COUNT * PAGE_POSITIONS, KEY_VALUE_HEADS, 2, HEAD_SIZE)
            return attend(query_rows, key_rows, value_rows, page_row_entries[:, :, 0], page_row_entries[:, :, 1], key_spots < length)
        packed_pages = (query_vectors.reshape(REQUEST_COUNT, BLOCK_TOKENS, KEY_VALUE_HEADS, heads_per_group, HEAD_SIZE), block_keys.reshape(REQUEST_COUNT, BLOCK_TOKENS, KEY_VALUE_HEADS, HEAD_SIZE), block_values.reshape(REQUEST_COUNT, BLOCK_TOKENS, KEY_VALUE_HEADS, HEAD_SIZE), page_owner_device, cached_length, jnp.arange(REQUEST_COUNT, dtype=jnp.int32))
        results.append(lax.map(request, packed_pages).reshape(TOKENS, QUERY_HEADS * HEAD_SIZE))
    return (results[0], results[1])
```

```python
import functools
import math

import jax
import jax.numpy as jnp
from jax import lax
from jax.experimental import pallas as pl
from jax.experimental.pallas import tpu as pltpu
from jax.sharding import PartitionSpec as P

QUERY_HEADS = 32
KEY_VALUE_HEADS = 8
HEAD_SIZE = 128
HEADS_PER_GROUP = QUERY_HEADS // KEY_VALUE_HEADS
ACCEPTED = 32
THETA = 500000.0
MASKED = -1e30
SCALE = math.log2(math.e) / math.sqrt(HEAD_SIZE)
MESH = pl.DeviceIdType.MESH


def kernel(
    members, heads, inner,
    page_ref, length_ref, emb_ref, gain_ref, cos_ref, sin_ref, ids_ref, sel_ref, accept_ref,
    w_hbm, table_hbm, pages_hbm,
    out1_ref, out2_ref,
    w, table, pages, x2, normed, q, kb, vb, top, total, acc,
    ids_all, found_acc, found, recv_a, sum_a, recv_b, rows,
    w_sem, table_sem, own_sem, page_send, page_recv, ids_send, ids_recv,
    a_send, a_recv, b_send, b_recv, h_send, h_recv,
):
    me = lax.axis_index("tok")
    my_head = lax.axis_index("head")
    outer = members // inner
    my_outer, my_inner = me // inner, lax.rem(me, inner)
    groups = w.shape[1] // ((HEADS_PER_GROUP + 2) * HEAD_SIZE)
    length = emb_ref.shape[0]
    slots, width = found.shape[2], found.shape[3]
    page_size = pages.shape[1]
    q_rows = HEADS_PER_GROUP * length

    def tok_peer(step):
        return lax.rem(me + step, members)

    def tok_source(step):
        return lax.rem(me - step + members, members)

    def page_copy(step):
        peer = tok_peer(step)
        return pltpu.make_async_remote_copy(
            src_ref=pages_hbm.at[0, peer], dst_ref=pages.at[me],
            send_sem=page_send.at[peer], recv_sem=page_recv.at[me],
            device_id={"tok": peer}, device_id_type=MESH,
        )

    def page_arrival(source):
        return pltpu.make_async_remote_copy(
            src_ref=pages_hbm.at[0, source], dst_ref=pages.at[source],
            send_sem=page_send.at[source], recv_sem=page_recv.at[source],
            device_id={"tok": source}, device_id_type=MESH,
        )

    def ids_copy(peer, slot):
        return pltpu.make_async_remote_copy(
            src_ref=ids_ref, dst_ref=ids_all.at[slot],
            send_sem=ids_send.at[peer], recv_sem=ids_recv.at[slot],
            device_id={"tok": peer}, device_id_type=MESH,
        )

    def a_copy(other, slot):
        return pltpu.make_async_remote_copy(
            src_ref=found.at[:, other], dst_ref=recv_a.at[slot],
            send_sem=a_send.at[other], recv_sem=a_recv.at[slot],
            device_id={"tok": my_outer * inner + other}, device_id_type=MESH,
        )

    def b_copy(other, slot):
        return pltpu.make_async_remote_copy(
            src_ref=sum_a.at[other], dst_ref=recv_b.at[slot],
            send_sem=b_send.at[other], recv_sem=b_recv.at[slot],
            device_id={"tok": other * inner + my_inner}, device_id_type=MESH,
        )

    def h_copy(other, slot):
        return pltpu.make_async_remote_copy(
            src_ref=rows.at[my_head], dst_ref=rows.at[slot],
            send_sem=h_send.at[other], recv_sem=h_recv.at[slot],
            device_id={"head": other}, device_id_type=MESH,
        )

    table_chunk = table.shape[0] // table_sem.shape[0]

    def table_copy(i):
        part = pl.ds(pl.multiple_of(i * table_chunk, table_chunk), table_chunk)
        return pltpu.make_async_copy(table_hbm.at[part], table.at[part], table_sem.at[i])

    def w_copy(i):
        part = pl.ds(i * 2 * HEAD_SIZE, 2 * HEAD_SIZE)
        return pltpu.make_async_copy(w_hbm.at[:, part], w.at[:, part], w_sem.at[i])

    own_copy = pltpu.make_async_copy(pages_hbm.at[0, me], pages.at[me], own_sem)

    @pl.loop(0, table_sem.shape[0])
    def _(i):
        table_copy(i).start()

    barrier = pltpu.get_barrier_semaphore()

    @pl.loop(1, members)
    def _(step):
        pl.semaphore_signal(
            barrier, inc=1, device_id={"tok": tok_peer(step)}, device_id_type=MESH
        )

    @pl.loop(1, heads)
    def _(step):
        pl.semaphore_signal(
            barrier, inc=1, device_id={"head": lax.rem(my_head + step, heads)},
            device_id_type=MESH,
        )

    pl.semaphore_wait(barrier, members - 1 + heads - 1)

    @pl.loop(1, members)
    def _(step):
        ids_copy(tok_peer(step), me).start()

    @pl.loop(1, members)
    def _(step):
        page_copy(step).start()

    for i in range(3 * groups):
        w_copy(i).start()
    own_copy.start()
    ids_all[me] = ids_ref[...]

    def normalize(x_ref):
        @pl.loop(0, length // 16)
        def _(i):
            part = pl.ds(pl.multiple_of(i * 16, 16), 16)
            x = x_ref[part, :].astype(jnp.float32)
            inverse = lax.rsqrt(jnp.mean(x * x, axis=-1, keepdims=True) + 1e-05)
            normed[part, :] = (x * inverse * gain_ref[...].astype(jnp.float32)).astype(jnp.bfloat16)

    def rotated(v):
        return (v * cos_ref[...] + pltpu.roll(v, HEAD_SIZE // 2, 1) * sin_ref[...]).astype(
            jnp.bfloat16
        )

    def project(p):
        for g in range(groups):
            for c in range(3):
                i = g * 3 + c
                if p == 0:
                    w_copy(i).wait()
                y = jnp.dot(
                    normed[...], w[:, i * 256 : (i + 1) * 256], preferred_element_type=jnp.float32
                )
                left, right = y[:, :HEAD_SIZE], y[:, HEAD_SIZE:]
                if c < 2:
                    row = 2 * c * length
                    q[p, g, row : row + length, :] = rotated(left)
                    q[p, g, row + length : row + 2 * length, :] = rotated(right)
                else:
                    kb[p, g] = rotated(left)
                    vb[p, g] = right.astype(jnp.bfloat16)

    def scores_of(keys, p, g):
        return SCALE * lax.dot_general(
            keys, q[p, g], (((1,), (1,)), ((), ())), preferred_element_type=jnp.float32
        )

    def weighted(values, weights):
        return lax.dot_general(
            values, weights.astype(jnp.bfloat16), (((0,), (0,)), ((), ())),
            preferred_element_type=jnp.float32,
        )

    def attend_block(p):
        for g in range(groups):
            s = scores_of(kb[p, g], p, g)
            high = jnp.max(s, axis=0, keepdims=True)
            e = jnp.exp2(s - high)
            top[p, g] = high
            total[p, g] = jnp.sum(e, axis=0, keepdims=True)
            acc[p, g] = weighted(vb[p, g], e)

    def attend_page(source, p):
        limit = length_ref[0] - page_ref[0, source] * page_size
        usable = lax.broadcasted_iota(jnp.int32, (page_size, q_rows), 0) < limit
        for g in range(groups):
            keys = pages[source, :, g * 256 : g * 256 + 128]
            values = pages[source, :, g * 256 + 128 : g * 256 + 256]
            s = jnp.where(usable, scores_of(keys, p, g), MASKED)
            before = top[p, g]
            high = jnp.maximum(before, jnp.max(s, axis=0, keepdims=True))
            shrink = jnp.exp2(before - high)
            e = jnp.exp2(s - high)
            top[p, g] = high
            total[p, g] = total[p, g] * shrink + jnp.sum(e, axis=0, keepdims=True)
            acc[p, g] = acc[p, g] * shrink + weighted(values, e)

    normalize(emb_ref)

    @pl.loop(1, members)
    def _(step):
        source = tok_source(step)
        ids_copy(source, source).wait_recv()

    found_acc[...] = jnp.zeros_like(found_acc)
    wanted = ids_all[...].reshape(members * slots, HEAD_SIZE)[:, :1] - me * table.shape[0]

    @pl.loop(0, table_sem.shape[0])
    def _(i):
        table_copy(i).wait()
        spots = lax.broadcasted_iota(jnp.int32, (members * slots, table_chunk), 1)
        hot = jnp.where(wanted - i * table_chunk == spots, 1.0, 0.0).astype(jnp.bfloat16)
        part = pl.ds(pl.multiple_of(i * table_chunk, table_chunk), table_chunk)
        found_acc[...] += jnp.dot(hot, table[part, :], preferred_element_type=jnp.float32)

    for m in range(members):
        found[m // inner, m % inner] = found_acc[m * slots : (m + 1) * slots, :].astype(jnp.bfloat16)

    @pl.loop(1, inner)
    def _(step):
        a_copy(lax.rem(my_inner + step, inner), my_inner).start()

    project(0)

    sum_a[...] = found[:, my_inner]

    @pl.loop(1, inner)
    def _(step):
        source = lax.rem(my_inner - step + inner, inner)
        a_copy(source, source).wait_recv()
        sum_a[...] += recv_a[source]

    @pl.loop(1, outer)
    def _(step):
        b_copy(lax.rem(my_outer + step, outer), my_outer).start()

    attend_block(0)
    rows[my_head] = sum_a[my_outer]

    @pl.loop(1, outer)
    def _(step):
        source = lax.rem(my_outer - step + outer, outer)
        b_copy(source, source).wait_recv()
        rows[my_head] += recv_b[source]

    @pl.loop(1, heads)
    def _(step):
        h_copy(lax.rem(my_head + step, heads), my_head).start()

    own_copy.wait()
    attend_page(me, 0)

    @pl.loop(1, heads)
    def _(step):
        source = lax.rem(my_head - step + heads, heads)
        h_copy(source, source).wait_recv()

    for h in range(heads):
        part = slice(h * width, (h + 1) * width)
        placed = jnp.dot(sel_ref[...], rows[h], preferred_element_type=jnp.float32)
        x2[:, part] = jnp.where(
            accept_ref[...] == 1, placed, emb_ref[:, part].astype(jnp.float32)
        ).astype(jnp.bfloat16)
    normalize(x2)
    project(1)
    attend_block(1)
    attend_page(me, 1)

    @pl.loop(1, members)
    def _(step):
        source = tok_source(step)
        page_arrival(source).wait_recv()
        attend_page(source, 0)
        attend_page(source, 1)

    for p, out in enumerate((out1_ref, out2_ref)):
        for g in range(groups):
            result = acc[p, g] / total[p, g]
            for h in range(HEADS_PER_GROUP):
                column = (g * HEADS_PER_GROUP + h) * HEAD_SIZE
                out[:, column : column + HEAD_SIZE] = result[
                    :, h * length : (h + 1) * length
                ].T.astype(jnp.bfloat16)

    @pl.loop(1, members)
    def _(step):
        ids_copy(tok_peer(step), me).wait_send()
        page_copy(step).wait_send()

    @pl.loop(1, inner)
    def _(step):
        a_copy(lax.rem(my_inner + step, inner), my_inner).wait_send()

    @pl.loop(1, outer)
    def _(step):
        b_copy(lax.rem(my_outer + step, outer), my_outer).wait_send()

    @pl.loop(1, heads)
    def _(step):
        h_copy(lax.rem(my_head + step, heads), my_head).wait_send()


def body(
    embeddings, norm_gain, query_key_value_weight, embed_table, rotated_cache_pages,
    page_owner_device, cached_length, vocab_shard, shard_row, accept,
):
    members = lax.axis_size("tok")
    heads = lax.axis_size("head")
    inner = 1
    while 4 * inner * inner <= members:
        inner *= 2
    outer = members // inner
    length, model = embeddings.shape
    columns = query_key_value_weight.shape[1]
    shard_rows, width = embed_table.shape
    page_size = rotated_cache_pages.shape[2]
    groups = columns // ((HEADS_PER_GROUP + 2) * HEAD_SIZE)
    slots = ACCEPTED
    q_rows = HEADS_PER_GROUP * length

    positions = (cached_length[0] + jnp.arange(length, dtype=jnp.int32)).astype(jnp.float32)
    halves = jnp.arange(HEAD_SIZE, dtype=jnp.int32) % (HEAD_SIZE // 2)
    frequency = THETA ** (-(halves.astype(jnp.float32) * 2.0) / HEAD_SIZE)
    turning = positions[:, None] * frequency[None, :]
    sign = jnp.where(jnp.arange(HEAD_SIZE) < HEAD_SIZE // 2, -1.0, 1.0)
    cosine, sine = jnp.cos(turning), jnp.sin(turning) * sign[None, :]

    sources = jnp.arange(members, dtype=jnp.int32)
    page_index = jnp.sum(
        jnp.where(page_owner_device[0][:, None] == sources[None, :], sources[:, None], 0), axis=0
    )[None, :]
    token_ids = vocab_shard[:, 0] * shard_rows + shard_row
    order = jnp.arange(length)
    earlier = jnp.sum(
        jnp.where(order[None, :] < order[:, None], accept[None, :], 0), axis=1
    )
    selected = (accept[:, None] == 1) & (earlier[:, None] == jnp.arange(slots)[None, :])
    slot_ids = jnp.sum(jnp.where(selected, token_ids[:, None], 0), axis=0)
    slot_ids = jnp.broadcast_to(slot_ids[:, None], (slots, 128)).astype(jnp.int32)

    vmem = pl.BlockSpec(memory_space=pltpu.VMEM)
    smem = pl.BlockSpec(memory_space=pltpu.SMEM)
    anywhere = pl.BlockSpec(memory_space=pl.ANY)
    bf16, f32 = jnp.bfloat16, jnp.float32
    table_chunks = max(1, shard_rows // 1024)
    dma = pltpu.SemaphoreType.DMA
    return pl.pallas_call(
        functools.partial(kernel, members, heads, inner),
        out_shape=(
            jax.ShapeDtypeStruct((length, groups * q_rows), bf16),
            jax.ShapeDtypeStruct((length, groups * q_rows), bf16),
        ),
        in_specs=[smem, smem] + [vmem] * 7 + [anywhere] * 3,
        out_specs=(vmem, vmem),
        scratch_shapes=[
            pltpu.VMEM((model, columns), bf16),
            pltpu.VMEM((shard_rows, width), bf16),
            pltpu.VMEM((members, page_size, rotated_cache_pages.shape[3]), bf16),
            pltpu.VMEM((length, model), bf16),
            pltpu.VMEM((length, model), bf16),
            pltpu.VMEM((2, groups, q_rows, HEAD_SIZE), bf16),
            pltpu.VMEM((2, groups, length, HEAD_SIZE), bf16),
            pltpu.VMEM((2, groups, length, HEAD_SIZE), bf16),
            pltpu.VMEM((2, groups, 1, q_rows), f32),
            pltpu.VMEM((2, groups, 1, q_rows), f32),
            pltpu.VMEM((2, groups, HEAD_SIZE, q_rows), f32),
            pltpu.VMEM((members, slots, 128), jnp.int32),
            pltpu.VMEM((members * slots, width), f32),
            pltpu.VMEM((outer, inner, slots, width), bf16),
            pltpu.VMEM((inner, outer, slots, width), bf16),
            pltpu.VMEM((outer, slots, width), bf16),
            pltpu.VMEM((outer, slots, width), bf16),
            pltpu.VMEM((heads, slots, width), bf16),
            dma((3 * groups,)),
            dma((table_chunks,)),
            dma,
            dma((members,)), dma((members,)), dma((members,)), dma((members,)),
            dma((inner,)), dma((inner,)), dma((outer,)), dma((outer,)),
            dma((heads,)), dma((heads,)),
        ],
        compiler_params=pltpu.CompilerParams(
            collective_id=0, has_side_effects=True, vmem_limit_bytes=56 * 2**20
        ),
    )(
        page_index, cached_length, embeddings, norm_gain[None, :], cosine, sine, slot_ids,
        selected.astype(bf16), accept[:, None],
        query_key_value_weight, embed_table, rotated_cache_pages,
    )


def solution(mesh):
    return jax.shard_map(
        body,
        mesh=mesh,
        in_specs=(
            P("tok", None),
            P(),
            P(None, "head"),
            P("tok", "head"),
            P("tok", None, None, "head"),
            P("tok", None),
            P("tok"),
            P("tok", None),
            P("tok"),
            P("tok"),
        ),
        out_specs=(P("tok", "head"), P("tok", "head")),
        check_vma=False,
    )
```

```python
import functools
import math

import jax
import jax.numpy as jnp
from jax import lax
from jax.experimental import pallas as pl
from jax.experimental.pallas import tpu as pltpu
from jax.sharding import PartitionSpec as P

QUERY_HEADS = 32
KEY_VALUE_HEADS = 8
HEAD_SIZE = 128
HEADS_PER_GROUP = QUERY_HEADS // KEY_VALUE_HEADS
ACCEPTED = 32
THETA = 500000.0
MASKED = -1e30
SCALE = math.log2(math.e) / math.sqrt(HEAD_SIZE)
MESH = pl.DeviceIdType.MESH


def kernel(
    members, heads, inner,
    owner_ref, length_ref, emb_ref, gain_ref, cos_ref, sin_ref, wanted_ref, accept_ref,
    w_hbm, table_hbm, pages_hbm,
    out1_ref, out2_ref,
    w, table, pages, x2, normed, q, kb, vb, top, total, acc,
    ids_ref, ids_all, found_acc, found, recv_a, sum_a, recv_b, rows,
    w_sem, table_sem, own_sem, page_send, page_recv, ids_send, ids_recv,
    a_send, a_recv, b_send, b_recv, h_send, h_recv,
):
    me = lax.axis_index("tok")
    my_head = lax.axis_index("head")
    outer = members // inner
    my_outer, my_inner = me // inner, lax.rem(me, inner)
    groups = w.shape[1] // ((HEADS_PER_GROUP + 2) * HEAD_SIZE)
    length = emb_ref.shape[0]
    slots, width = found.shape[2], found.shape[3]
    page_size = pages.shape[1]
    q_rows = HEADS_PER_GROUP * length

    def tok_peer(step):
        return lax.rem(me + step, members)

    def tok_source(step):
        return lax.rem(me - step + members, members)

    def crossed(step):
        peer, bit = me, 1
        while bit < members:
            peer = peer + lax.rem(step // bit, 2) * bit * (1 - 2 * lax.rem(me // bit, 2))
            bit *= 2
        return peer

    def page_copy(step):
        peer = crossed(step)
        return pltpu.make_async_remote_copy(
            src_ref=pages_hbm.at[0, peer], dst_ref=pages.at[me],
            send_sem=page_send.at[peer], recv_sem=page_recv.at[me],
            device_id={"tok": peer}, device_id_type=MESH,
        )

    def page_arrival(source):
        return pltpu.make_async_remote_copy(
            src_ref=pages_hbm.at[0, source], dst_ref=pages.at[source],
            send_sem=page_send.at[source], recv_sem=page_recv.at[source],
            device_id={"tok": source}, device_id_type=MESH,
        )

    def ids_copy(peer, slot):
        return pltpu.make_async_remote_copy(
            src_ref=ids_ref, dst_ref=ids_all.at[slot],
            send_sem=ids_send.at[peer], recv_sem=ids_recv.at[slot],
            device_id={"tok": peer}, device_id_type=MESH,
        )

    def a_copy(other, slot):
        return pltpu.make_async_remote_copy(
            src_ref=found.at[:, other], dst_ref=recv_a.at[slot],
            send_sem=a_send.at[other], recv_sem=a_recv.at[slot],
            device_id={"tok": my_outer * inner + other}, device_id_type=MESH,
        )

    def b_copy(other, slot):
        return pltpu.make_async_remote_copy(
            src_ref=sum_a.at[other], dst_ref=recv_b.at[slot],
            send_sem=b_send.at[other], recv_sem=b_recv.at[slot],
            device_id={"tok": other * inner + my_inner}, device_id_type=MESH,
        )

    def h_copy(other, slot):
        return pltpu.make_async_remote_copy(
            src_ref=rows.at[my_head], dst_ref=rows.at[slot],
            send_sem=h_send.at[other], recv_sem=h_recv.at[slot],
            device_id={"head": other}, device_id_type=MESH,
        )

    table_chunk = table.shape[0] // table_sem.shape[0]

    def table_copy(i):
        part = pl.ds(pl.multiple_of(i * table_chunk, table_chunk), table_chunk)
        return pltpu.make_async_copy(table_hbm.at[part], table.at[part], table_sem.at[i])

    def w_copy(i):
        part = pl.ds(i * 2 * HEAD_SIZE, 2 * HEAD_SIZE)
        return pltpu.make_async_copy(w_hbm.at[:, part], w.at[:, part], w_sem.at[i])

    half = members // 2
    quarter = members // 4

    def send_pages(part):
        if part == "far0":
            lo, hi = half, half + quarter
        elif part == "far1":
            lo, hi = half + quarter, members
        elif part == "near":
            lo, hi = 1, half
        else:
            lo, hi = 1, 1

        @pl.loop(lo, hi)
        def _(step):
            page_copy(step).start()

    own_copy = pltpu.make_async_copy(pages_hbm.at[0, me], pages.at[me], own_sem)

    @pl.loop(0, table_sem.shape[0])
    def _(i):
        table_copy(i).start()

    taken = accept_ref[...]
    before_of = lax.broadcasted_iota(jnp.int32, (length, length), 0) < lax.broadcasted_iota(
        jnp.int32, (length, length), 1
    )
    earlier = jnp.dot(
        taken.astype(jnp.float32).astype(jnp.bfloat16),
        jnp.where(before_of, 1.0, 0.0).astype(jnp.bfloat16),
        preferred_element_type=jnp.float32,
    ).astype(jnp.int32)
    slot_of = lax.broadcasted_iota(jnp.int32, (slots, length), 0)
    selected = (earlier == slot_of) & (taken == 1)
    ids_ref[...] = jnp.broadcast_to(
        jnp.sum(jnp.where(selected, wanted_ref[...], 0), axis=1, keepdims=True), ids_ref.shape
    )

    barrier = pltpu.get_barrier_semaphore()

    @pl.loop(1, members)
    def _(step):
        pl.semaphore_signal(
            barrier, inc=1, device_id={"tok": tok_peer(step)}, device_id_type=MESH
        )

    @pl.loop(1, heads)
    def _(step):
        pl.semaphore_signal(
            barrier, inc=1, device_id={"head": lax.rem(my_head + step, heads)},
            device_id_type=MESH,
        )

    pl.semaphore_wait(barrier, members - 1 + heads - 1)

    @pl.loop(1, members)
    def _(step):
        ids_copy(tok_peer(step), me).start()

    send_pages("far0")
    send_pages("near")
    send_pages("far1")

    for i in range(3 * groups):
        w_copy(i).start()
    own_copy.start()
    ids_all[me] = ids_ref[...]

    def normalize(x_ref):
        @pl.loop(0, length // 16)
        def _(i):
            part = pl.ds(pl.multiple_of(i * 16, 16), 16)
            x = x_ref[part, :].astype(jnp.float32)
            inverse = lax.rsqrt(jnp.mean(x * x, axis=-1, keepdims=True) + 1e-05)
            normed[part, :] = (x * inverse * gain_ref[...].astype(jnp.float32)[None, :]).astype(jnp.bfloat16)

    def rotated(v):
        return (v * cos_ref[...] + pltpu.roll(v, HEAD_SIZE // 2, 1) * sin_ref[...]).astype(
            jnp.bfloat16
        )

    def project(p):
        for g in range(groups):
            for c in range(3):
                i = g * 3 + c
                if p == 0:
                    w_copy(i).wait()
                y = jnp.dot(
                    normed[...], w[:, i * 256 : (i + 1) * 256], preferred_element_type=jnp.float32
                )
                left, right = y[:, :HEAD_SIZE], y[:, HEAD_SIZE:]
                if c < 2:
                    row = 2 * c * length
                    q[p, g, row : row + length, :] = rotated(left)
                    q[p, g, row + length : row + 2 * length, :] = rotated(right)
                else:
                    kb[p, g] = rotated(left)
                    vb[p, g] = right.astype(jnp.bfloat16)

    def scores_of(keys, p, g):
        return SCALE * lax.dot_general(
            keys, q[p, g], (((1,), (1,)), ((), ())), preferred_element_type=jnp.float32
        )

    def weighted(values, weights):
        return lax.dot_general(
            values, weights.astype(jnp.bfloat16), (((0,), (0,)), ((), ())),
            preferred_element_type=jnp.float32,
        )

    def attend_block(p):
        for g in range(groups):
            s = scores_of(kb[p, g], p, g)
            high = jnp.max(s, axis=0, keepdims=True)
            e = jnp.exp2(s - high)
            top[p, g] = high
            total[p, g] = jnp.sum(e, axis=0, keepdims=True)
            acc[p, g] = weighted(vb[p, g], e)

    def attend_page(source, p):
        index = jnp.int32(0)
        for i in range(members):
            index = index + jnp.where(owner_ref[0, i] == source, i, 0)
        limit = length_ref[0] - index * page_size
        usable = lax.broadcasted_iota(jnp.int32, (page_size, q_rows), 0) < limit
        for g in range(groups):
            keys = pages[source, :, g * 256 : g * 256 + 128]
            values = pages[source, :, g * 256 + 128 : g * 256 + 256]
            s = jnp.where(usable, scores_of(keys, p, g), MASKED)
            before = top[p, g]
            high = jnp.maximum(before, jnp.max(s, axis=0, keepdims=True))
            shrink = jnp.exp2(before - high)
            e = jnp.exp2(s - high)
            top[p, g] = high
            total[p, g] = total[p, g] * shrink + jnp.sum(e, axis=0, keepdims=True)
            acc[p, g] = acc[p, g] * shrink + weighted(values, e)

    normalize(emb_ref)

    @pl.loop(1, members)
    def _(step):
        source = tok_source(step)
        ids_copy(source, source).wait_recv()

    found_acc[...] = jnp.zeros_like(found_acc)
    wanted = ids_all[...].reshape(members * slots, HEAD_SIZE)[:, :1] - me * table.shape[0]

    @pl.loop(0, table_sem.shape[0])
    def _(i):
        table_copy(i).wait()
        spots = lax.broadcasted_iota(jnp.int32, (members * slots, table_chunk), 1)
        hot = jnp.where(wanted - i * table_chunk == spots, 1.0, 0.0).astype(jnp.bfloat16)
        part = pl.ds(pl.multiple_of(i * table_chunk, table_chunk), table_chunk)
        found_acc[...] += jnp.dot(hot, table[part, :], preferred_element_type=jnp.float32)

    for m in range(members):
        found[m // inner, m % inner] = found_acc[m * slots : (m + 1) * slots, :].astype(jnp.bfloat16)

    @pl.loop(1, inner)
    def _(step):
        a_copy(lax.rem(my_inner + step, inner), my_inner).start()

    project(0)
    attend_block(0)
    own_copy.wait()
    attend_page(me, 0)

    sum_a[...] = found[:, my_inner]

    @pl.loop(1, inner)
    def _(step):
        source = lax.rem(my_inner - step + inner, inner)
        a_copy(source, source).wait_recv()
        sum_a[...] += recv_a[source]

    @pl.loop(1, outer)
    def _(step):
        b_copy(lax.rem(my_outer + step, outer), my_outer).start()

    rows[my_head] = sum_a[my_outer]

    @pl.loop(1, half)
    def _(step):
        source = crossed(step)
        page_arrival(source).wait_recv()
        attend_page(source, 0)

    @pl.loop(1, outer)
    def _(step):
        source = lax.rem(my_outer - step + outer, outer)
        b_copy(source, source).wait_recv()
        rows[my_head] += recv_b[source]

    @pl.loop(1, heads)
    def _(step):
        h_copy(lax.rem(my_head + step, heads), my_head).start()

    @pl.loop(half, half + quarter)
    def _(step):
        source = crossed(step)
        page_arrival(source).wait_recv()
        attend_page(source, 0)

    @pl.loop(1, heads)
    def _(step):
        source = lax.rem(my_head - step + heads, heads)
        h_copy(source, source).wait_recv()

    chosen = jnp.where(selected, 1.0, 0.0).astype(jnp.bfloat16)
    replaces = lax.dot_general(
        chosen, jnp.ones((slots, HEAD_SIZE), jnp.bfloat16), (((0,), (0,)), ((), ())),
        preferred_element_type=jnp.float32,
    )[:, :1] > 0.5
    for h in range(heads):
        part = slice(h * width, (h + 1) * width)
        placed = lax.dot_general(
            chosen, rows[h], (((0,), (0,)), ((), ())), preferred_element_type=jnp.float32
        )
        x2[:, part] = jnp.where(
            replaces, placed, emb_ref[:, part].astype(jnp.float32)
        ).astype(jnp.bfloat16)
    normalize(x2)
    project(1)
    attend_block(1)
    attend_page(me, 1)

    @pl.loop(1, half + quarter)
    def _(step):
        attend_page(crossed(step), 1)

    @pl.loop(half + quarter, members)
    def _(step):
        source = crossed(step)
        page_arrival(source).wait_recv()
        attend_page(source, 0)
        attend_page(source, 1)

    for p, out in enumerate((out1_ref, out2_ref)):
        for g in range(groups):
            result = acc[p, g] / total[p, g]
            for h in range(HEADS_PER_GROUP):
                column = (g * HEADS_PER_GROUP + h) * HEAD_SIZE
                out[:, column : column + HEAD_SIZE] = result[
                    :, h * length : (h + 1) * length
                ].T.astype(jnp.bfloat16)

    @pl.loop(1, members)
    def _(step):
        ids_copy(tok_peer(step), me).wait_send()
        page_copy(step).wait_send()

    @pl.loop(1, inner)
    def _(step):
        a_copy(lax.rem(my_inner + step, inner), my_inner).wait_send()

    @pl.loop(1, outer)
    def _(step):
        b_copy(lax.rem(my_outer + step, outer), my_outer).wait_send()

    @pl.loop(1, heads)
    def _(step):
        h_copy(lax.rem(my_head + step, heads), my_head).wait_send()


def body(
    embeddings, norm_gain, query_key_value_weight, embed_table, rotated_cache_pages,
    page_owner_device, cached_length, vocab_shard, shard_row, accept,
):
    members = lax.axis_size("tok")
    heads = lax.axis_size("head")
    inner = 1
    while 4 * inner * inner <= members:
        inner *= 2
    outer = members // inner
    length, model = embeddings.shape
    columns = query_key_value_weight.shape[1]
    shard_rows, width = embed_table.shape
    page_size = rotated_cache_pages.shape[2]
    groups = columns // ((HEADS_PER_GROUP + 2) * HEAD_SIZE)
    slots = ACCEPTED
    q_rows = HEADS_PER_GROUP * length

    positions = (cached_length[0] + jnp.arange(length, dtype=jnp.int32)).astype(jnp.float32)
    halves = jnp.arange(HEAD_SIZE, dtype=jnp.int32) % (HEAD_SIZE // 2)
    frequency = THETA ** (-(halves.astype(jnp.float32) * 2.0) / HEAD_SIZE)
    turning = positions[:, None] * frequency[None, :]
    sign = jnp.where(jnp.arange(HEAD_SIZE) < HEAD_SIZE // 2, -1.0, 1.0)
    cosine, sine = jnp.cos(turning), jnp.sin(turning) * sign[None, :]

    token_ids = (vocab_shard[:, 0] * shard_rows + shard_row)[None, :]

    vmem = pl.BlockSpec(memory_space=pltpu.VMEM)
    smem = pl.BlockSpec(memory_space=pltpu.SMEM)
    anywhere = pl.BlockSpec(memory_space=pl.ANY)
    bf16, f32 = jnp.bfloat16, jnp.float32
    table_chunks = max(1, shard_rows // 1024)
    dma = pltpu.SemaphoreType.DMA
    return pl.pallas_call(
        functools.partial(kernel, members, heads, inner),
        out_shape=(
            jax.ShapeDtypeStruct((length, groups * q_rows), bf16),
            jax.ShapeDtypeStruct((length, groups * q_rows), bf16),
        ),
        in_specs=[smem, smem] + [vmem] * 6 + [anywhere] * 3,
        out_specs=(vmem, vmem),
        scratch_shapes=[
            pltpu.VMEM((model, columns), bf16),
            pltpu.VMEM((shard_rows, width), bf16),
            pltpu.VMEM((members, page_size, rotated_cache_pages.shape[3]), bf16),
            pltpu.VMEM((length, model), bf16),
            pltpu.VMEM((length, model), bf16),
            pltpu.VMEM((2, groups, q_rows, HEAD_SIZE), bf16),
            pltpu.VMEM((2, groups, length, HEAD_SIZE), bf16),
            pltpu.VMEM((2, groups, length, HEAD_SIZE), bf16),
            pltpu.VMEM((2, groups, 1, q_rows), f32),
            pltpu.VMEM((2, groups, 1, q_rows), f32),
            pltpu.VMEM((2, groups, HEAD_SIZE, q_rows), f32),
            pltpu.VMEM((slots, 128), jnp.int32),
            pltpu.VMEM((members, slots, 128), jnp.int32),
            pltpu.VMEM((members * slots, width), f32),
            pltpu.VMEM((outer, inner, slots, width), bf16),
            pltpu.VMEM((inner, outer, slots, width), bf16),
            pltpu.VMEM((outer, slots, width), bf16),
            pltpu.VMEM((outer, slots, width), bf16),
            pltpu.VMEM((heads, slots, width), bf16),
            dma((3 * groups,)),
            dma((table_chunks,)),
            dma,
            dma((members,)), dma((members,)), dma((members,)), dma((members,)),
            dma((inner,)), dma((inner,)), dma((outer,)), dma((outer,)),
            dma((heads,)), dma((heads,)),
        ],
        compiler_params=pltpu.CompilerParams(
            collective_id=0, has_side_effects=True, vmem_limit_bytes=56 * 2**20
        ),
    )(
        page_owner_device, cached_length, embeddings, norm_gain, cosine, sine, token_ids,
        accept[None, :],
        query_key_value_weight, embed_table, rotated_cache_pages,
    )


def solution(mesh):
    return jax.shard_map(
        body,
        mesh=mesh,
        in_specs=(
            P("tok", None),
            P(),
            P(None, "head"),
            P("tok", "head"),
            P("tok", None, None, "head"),
            P("tok", None),
            P("tok"),
            P("tok", None),
            P("tok"),
            P("tok"),
        ),
        out_specs=(P("tok", "head"), P("tok", "head")),
        check_vma=False,
    )
```
